32 devices in a mesh: tm: 8 (over z, x), rows: 4 (over y, core).
Axes of the slice: x: 2, y: 2, z: 4, core: 2. Of those that a mesh axis runs over, the one named last changes fastest.
Arguments:
- frames: bfloat16 [8, 32, 32, 640], P('tm', 'rows'), may hold values from -24 to 24
- conv_weight: bfloat16 [3, 3, 640, 640], replicated, may hold values from -0.078125 to 0.078125
- conv_bias: float32 [640], replicated, may hold values from -1.5 to 1.5
- ref_features: bfloat16 [1024, 640], P('tm'), may hold values from -6 to 6
- w_query: bfloat16 [640, 640], replicated, may hold values from -0.25 to 0.25
- w_key: bfloat16 [640, 640], replicated, may hold values from -0.25 to 0.25
- w_value: bfloat16 [640, 640], replicated, may hold values from -0.25 to 0.25
- w_out: bfloat16 [640, 640], replicated, may hold values from -0.25 to 0.25
- out_bias: float32 [640], replicated, may hold values from -1.5 to 1.5
Outputs:
- hidden: bfloat16 [8, 32, 32, 640], P('tm', 'rows')
- attended: bfloat16 [8, 32, 32, 640], P('tm', 'rows')
The draws below stay inside these ranges and needn't reach their ends.
All inputs are finite; a program needn't handle non-finite values.
Results may differ from the reference program's by a relative error of at most 0.025.
Values may be sent and summed in bfloat16 or wider, within the bound.
No kernel may reach another device: no remote copies, remote signals or barrier semaphores. Data moves between devices by JAX's collectives and lax.ppermute only.
A program may use at most 128 MiB of HBM per device.

```python
import math
import jax
import jax.numpy as jnp
from jax import lax

H = 32
W = 32
HEADS = 8
HD = 80
C = 640
FRAMES = 8


def draw_frames(key, part):
    shape = (FRAMES, H, W, C)
    values = jnp.clip(jax.random.normal(jax.random.fold_in(key, 15), shape, jnp.float32), -6.0, 6.0)
    return values.astype(jnp.bfloat16)


def projection_parts(key):
    spread = 1.7 / math.sqrt(C)
    first = jnp.clip(jax.random.normal(jax.random.fold_in(key, 21), (C, C), jnp.float32), -6.0, 6.0) * spread
    second = jnp.clip(jax.random.normal(jax.random.fold_in(key, 22), (C, C), jnp.float32), -6.0, 6.0) * spread
    return (first, second)


def draw_w_query(key, part):
    first, second = projection_parts(key)
    return jnp.clip(first, -0.25, 0.25).astype(jnp.bfloat16)


def draw_w_key(key, part):
    first, second = projection_parts(key)
    values = second
    return jnp.clip(values, -0.25, 0.25).astype(jnp.bfloat16)


def shard_levels(rng, extent, pieces, smallest, largest):
    def one(position, shards_of):
        draws = jax.random.uniform(jax.random.fold_in(jax.random.fold_in(rng, 6), position), (shards_of,), jnp.float32, smallest / len(pieces), largest / len(pieces))
        return jnp.repeat(jnp.exp(draws), extent[position] // shards_of).reshape((-1,) + (1,) * (len(extent) - position - 1))

    loudness = one(*pieces[0])
    for cut in pieces[1:]:
        loudness = loudness * one(*cut)
    return loudness


def gaussian(key, dims, width, limit, pieces=(), held_as=jnp.bfloat16):
    level = shard_levels(key, dims, pieces, -0.22, 0.18) if pieces else 1.0
    entries = jax.random.normal(key, dims, jnp.float32) * width * level
    return jnp.minimum(jnp.maximum(entries, -limit), limit).astype(held_as)


def setup_inputs(seed: int = 0) -> dict:
    key_of = jax.random.split(jax.random.key(seed), 10)
    frames = draw_frames(jax.random.fold_in(key_of[9], 71), 0)
    conv_weight = gaussian(key_of[1], (3, 3, C, C), (9 * C) ** -0.5, 0.078125)
    conv_bias = gaussian(key_of[2], (C,), 0.3, 1.5, (), jnp.float32)
    ref_features = gaussian(key_of[3], (H * W, C), 1.0, 6.0, ((0, 8),))
    w_query = draw_w_query(jax.random.fold_in(key_of[9], 71), 0)
    w_key = draw_w_key(jax.random.fold_in(key_of[9], 71), 0)
    w_value = gaussian(key_of[6], (C, C), C ** -0.5, 0.25)
    w_out = gaussian(key_of[7], (C, C), C ** -0.5, 0.25)
    out_bias = gaussian(key_of[8], (C,), 0.3, 1.5, (), jnp.float32)
    return {"frames": frames, "conv_weight": conv_weight, "conv_bias": conv_bias, "ref_features": ref_features, "w_query": w_query, "w_key": w_key, "w_value": w_value, "w_out": w_out, "out_bias": out_bias}


def attend_head(query_head, key_head, value_head):
    scores = jnp.dot(query_head, key_head.T, preferred_element_type=jnp.float32) * (HD ** -0.5)
    top = jnp.max(scores, axis=1, keepdims=True)
    weights = jnp.exp(scores - top)
    total = jnp.sum(weights, axis=1, keepdims=True)
    summed = jnp.dot(weights.astype(jnp.bfloat16), value_head, preferred_element_type=jnp.float32)
    return summed / total


def reference(frames, conv_weight, conv_bias, ref_features, w_query, w_key, w_value, w_out, out_bias):
    ref_key = jnp.dot(ref_features, w_key, preferred_element_type=jnp.float32).astype(jnp.bfloat16)
    ref_value = jnp.dot(ref_features, w_value, preferred_element_type=jnp.float32).astype(jnp.bfloat16)

    def one_frame(latent):
        activated = jax.nn.silu(latent.astype(jnp.float32)).astype(jnp.bfloat16)
        padded = jnp.pad(activated, ((1, 1), (1, 1), (0, 0)))
        total = jnp.zeros((H * W, C), jnp.float32)
        for row_tap in range(3):
            for col_tap in range(3):
                window = padded[row_tap:row_tap + H, col_tap:col_tap + W].reshape(H * W, C)
                total = total + jnp.dot(window, conv_weight[row_tap, col_tap], preferred_element_type=jnp.float32)
        hidden = (latent.reshape(H * W, C).astype(jnp.float32) + total + conv_bias).astype(jnp.bfloat16)
        query = jnp.dot(hidden, w_query, preferred_element_type=jnp.float32).astype(jnp.bfloat16)
        key = jnp.dot(hidden, w_key, preferred_element_type=jnp.float32).astype(jnp.bfloat16)
        value = jnp.dot(hidden, w_value, preferred_element_type=jnp.float32).astype(jnp.bfloat16)
        keys = jnp.concatenate([key, ref_key], axis=0)
        values = jnp.concatenate([value, ref_value], axis=0)
        query_heads = query.reshape(H * W, HEADS, HD).transpose(1, 0, 2)
        key_heads = keys.reshape(2 * H * W, HEADS, HD).transpose(1, 0, 2)
        value_heads = values.reshape(2 * H * W, HEADS, HD).transpose(1, 0, 2)
        mixed = lax.map(lambda trio: attend_head(trio[0], trio[1], trio[2]), (query_heads, key_heads, value_heads))
        mixed = mixed.transpose(1, 0, 2).reshape(H * W, C).astype(jnp.bfloat16)
        attended = (jnp.dot(mixed, w_out, preferred_element_type=jnp.float32) + out_bias).astype(jnp.bfloat16)
        return hidden.reshape(H, W, C), attended.reshape(H, W, C)

    hidden, attended = lax.map(one_frame, frames)
    return hidden, attended
```

```python
import functools

import jax
import jax.numpy as jnp
from jax import lax
from jax.experimental import pallas as pl
from jax.experimental.pallas import tpu as pltpu
from jax.sharding import PartitionSpec as P

HD = 80
LANES = 128
SCALE = HD ** (-0.5) * 1.4426950408889634
BF = jnp.bfloat16
F32 = jnp.float32
VMEM_LIMIT = 24 << 20


def vmem_call(body, outs, scratch, *operands, flops=0):
    moved = sum(v.size * v.dtype.itemsize for v in list(operands) + jax.tree.leaves(outs))
    cost = pl.CostEstimate(flops=flops, bytes_accessed=moved, transcendentals=0)
    whole = pl.BlockSpec(memory_space=pltpu.VMEM)
    return pl.pallas_call(
        body,
        out_shape=outs,
        in_specs=[whole] * len(operands),
        out_specs=jax.tree.map(lambda _: whole, outs),
        scratch_shapes=scratch,
        cost_estimate=cost,
        compiler_params=pltpu.CompilerParams(vmem_limit_bytes=VMEM_LIMIT),
    )(*operands)


def silu(value):
    value = value.astype(F32)
    return value / (1.0 + jnp.exp(-value))


def opening_kernel(
    width, core, x_in, core_row, cross_row, weight_in, bias, wq_in, wk_in, wv_in, wo_in,
    hidden_out, hidden_work, query_out, wk_out, wv_out, wo_out,
    x, weight, square, shifted, wq, x_sem, weight_sem, square_sem,
):
    band, channels = x.shape
    heads = channels // HD
    x_copy = pltpu.make_async_copy(x_in, x, x_sem)
    square_copies = [
        pltpu.make_async_copy(source, square.at[i], square_sem.at[i])
        for i, source in enumerate((wk_in, wv_in, wq_in, wo_in))
    ]
    tap_copies = [
        pltpu.make_async_copy(weight_in.at[row], weight.at[row], weight_sem.at[row])
        for row in range(3)
    ]
    x_copy.start()
    for copy in square_copies:
        copy.start()
    wo_out[...] = jnp.zeros_like(wo_out)
    wq[...] = jnp.zeros_like(wq)
    is_first = core[0] == 0
    above = jnp.where(is_first, cross_row[...], core_row[...])
    below = jnp.where(is_first, core_row[...], cross_row[...])
    x_copy.wait()
    active = jnp.concatenate([silu(above), silu(x[...]), silu(below)], axis=0)
    rows = active.shape[0]
    column = lax.broadcasted_iota(jnp.int32, active.shape, 0) % width
    shifted[0] = jnp.where(column == 0, 0.0, pltpu.roll(active, 1, 0)).astype(BF)
    shifted[1] = active.astype(BF)
    shifted[2] = jnp.where(column == width - 1, 0.0, pltpu.roll(active, rows - 1, 0)).astype(BF)
    for copy in square_copies[:2]:
        copy.wait()
    tap_copies[0].start()
    wk_out[...] = square[0].T
    wv_out[...] = square[1].T
    for copy in square_copies[2:]:
        copy.wait()
    tap_copies[1].start()
    for head in range(heads):
        own, padded = slice(head * HD, (head + 1) * HD), slice(head * LANES, head * LANES + HD)
        wq[:, padded] = square[2, :, own]
        wo_out[padded, :] = square[3, own, :]
    total = x[...].astype(F32) + bias[...][None, :]
    for row in range(3):
        tap_copies[row].wait()
        if row == 0:
            tap_copies[2].start()
        for col in range(3):
            total = total + jnp.dot(
                shifted[col, row * width : row * width + band],
                weight[row, col],
                preferred_element_type=F32,
            )
    hidden = total.astype(BF)
    hidden_out[...] = hidden
    hidden_work[...] = hidden
    query_out[...] = (
        jnp.dot(hidden, wq[...], preferred_element_type=F32) * SCALE
    ).astype(BF)


def opening(core, x, core_row, cross_row, weight, bias, wq, wk, wv, wo, width):
    band, channels = x.shape
    heads = channels // HD
    shape = jax.ShapeDtypeStruct
    far = pl.BlockSpec(memory_space=pltpu.HBM)
    near = pl.BlockSpec(memory_space=pltpu.VMEM)
    outs = (
        shape((band, channels), BF),
        shape((band, channels), BF),
        shape((band, heads * LANES), BF),
        shape((channels, channels), BF),
        shape((channels, channels), BF),
        shape((heads * LANES, channels), BF),
    )
    x, weight, wq, wk, wv, wo = [
        pltpu.with_memory_space_constraint(v, pltpu.HBM) for v in (x, weight, wq, wk, wv, wo)
    ]
    return pl.pallas_call(
        functools.partial(opening_kernel, width),
        out_shape=outs,
        in_specs=[pl.BlockSpec(memory_space=pltpu.SMEM), far, near, near, far, near] + [far] * 4,
        out_specs=(near,) * len(outs),
        scratch_shapes=[
            pltpu.VMEM((band, channels), BF),
            pltpu.VMEM(weight.shape, BF),
            pltpu.VMEM((4, channels, channels), BF),
            pltpu.VMEM((3, band + 2 * width, channels), BF),
            pltpu.VMEM((channels, heads * LANES), BF),
            pltpu.SemaphoreType.DMA,
            pltpu.SemaphoreType.DMA((3,)),
            pltpu.SemaphoreType.DMA((4,)),
        ],
        cost_estimate=pl.CostEstimate(
            flops=18 * band * channels * channels, bytes_accessed=16 << 20, transcendentals=0
        ),
        compiler_params=pltpu.CompilerParams(vmem_limit_bytes=VMEM_LIMIT),
    )(core, x, core_row, cross_row, weight, bias, wq, wk, wv, wo)


def attend_kernel(pieces, first, last, *refs):
    refs = list(refs)
    sources = [refs.pop(0) for _ in range(pieces)]
    wk, wv, query = [refs.pop(0) for _ in range(3)]
    if not first:
        top_in, sum_in = refs.pop(0), refs.pop(0)
    if last:
        wo, bias, out, keys, values, mixed = refs
    else:
        top_out, sum_out, keys, values = refs
    channels = wk.shape[0]
    heads = channels // HD
    band = query.shape[0]
    tokens = keys.shape[1]
    keys[channels:, :] = jnp.zeros((keys.shape[0] - channels, tokens), BF)
    start = 0
    for source in sources:
        part = source[...]
        length = part.shape[0]
        here = slice(start, start + length)
        contract = (((1,), (1,)), ((), ()))
        keys[:channels, here] = lax.dot_general(
            wk[...], part, contract, preferred_element_type=F32
        ).astype(BF)
        value = lax.dot_general(wv[...], part, contract, preferred_element_type=F32).astype(BF)
        for head in range(heads):
            values[head * LANES : head * LANES + HD, here] = value[head * HD : (head + 1) * HD]
            values[head * LANES + HD : (head + 1) * LANES, here] = jnp.ones(
                (LANES - HD, length), BF
            )
        start += length

    def score(head):
        return jnp.dot(
            query[:, head * LANES : (head + 1) * LANES],
            keys[head * HD : head * HD + LANES, :],
            preferred_element_type=F32,
        )

    def weigh(scores, head):
        top = jnp.broadcast_to(jnp.max(scores, axis=1, keepdims=True), (band, LANES))
        if not first:
            top = jnp.maximum(top, top_in[head])
        weights = jnp.concatenate(
            [
                jnp.exp2(scores[:, at : at + LANES] - top).astype(BF)
                for at in range(0, tokens, LANES)
            ],
            axis=1,
        )
        return top, weights

    def finish(head, top, weights):
        product = lax.dot_general(
            weights,
            values[head * LANES : (head + 1) * LANES, :],
            (((1,), (1,)), ((), ())),
            preferred_element_type=F32,
        )
        if not first:
            product = product + sum_in[head] * jnp.exp2(top_in[head] - top)
        if last:
            mixed[:, head * LANES : (head + 1) * LANES] = (
                product / product[:, HD : HD + 1]
            ).astype(BF)
        else:
            top_out[head] = top
            sum_out[head] = product

    scores, ready = score(0), None
    for head in range(heads + 1):
        upcoming = score(head + 1) if head + 1 < heads else None
        weighed = weigh(scores, head) if head < heads else None
        if ready is not None:
            finish(head - 1, *ready)
        scores, ready = upcoming, weighed
    if last:
        out[...] = (
            jnp.dot(mixed[...], wo[...], preferred_element_type=F32) + bias[...][None, :]
        ).astype(BF)


def attend(sources, wk, wv, query, state=None, final=None):
    channels = wk.shape[0]
    heads = channels // HD
    band = query.shape[0]
    tokens = sum(source.shape[0] for source in sources)
    shape = jax.ShapeDtypeStruct
    scratch = [
        pltpu.VMEM((channels - HD + LANES, tokens), BF),
        pltpu.VMEM((heads * LANES, tokens), BF),
    ]
    operands = list(sources) + [wk, wv, query]
    if state is not None:
        operands += list(state)
    if final is not None:
        operands += list(final)
        outs = shape((band, channels), BF)
        scratch.append(pltpu.VMEM((band, heads * LANES), BF))
    else:
        outs = (shape((heads, band, LANES), F32), shape((heads, band, LANES), F32))
    return vmem_call(
        functools.partial(attend_kernel, len(sources), state is None, final is not None),
        outs,
        scratch,
        *operands,
        flops=4 * tokens * channels * (channels + 2 * band),
    )


def swap(value, axis, bit):
    size = lax.axis_size(axis)
    return lax.ppermute(value, axis, [(i, i ^ bit) for i in range(size)])


def shards(frames, conv_weight, conv_bias, ref_features, w_query, w_key, w_value, w_out, out_bias):
    count, band_rows, width, channels = frames.shape
    band = band_rows * width
    x = frames.reshape(count * band, channels)
    core = (lax.axis_index("rows") % 2).reshape(1).astype(jnp.int32)
    is_first = core[0] == 0
    first_row, last_row = x[:width], x[band - width :]
    between = [(i, i + 1) for i in range(1, lax.axis_size("rows") - 1, 2)]
    cross_row = lax.ppermute(
        jnp.where(is_first, first_row, last_row), "rows", between + [(j, i) for i, j in between]
    )
    core_row = swap(jnp.where(is_first, last_row, first_row), "rows", 1)
    half = ref_features.shape[0] // 2
    gathered = lax.dynamic_slice_in_dim(ref_features, core[0] * half, half, 0)
    bit = lax.axis_size("tm") // 2
    received = swap(gathered, "tm", bit)
    hidden_final, hidden, query, wk, wv, wo = opening(
        core,
        x,
        core_row,
        cross_row,
        conv_weight,
        conv_bias,
        w_query,
        w_key,
        w_value,
        w_out,
        width,
    )
    received, hidden = lax.optimization_barrier((received, hidden))
    hidden_y = swap(hidden, "rows", 2)
    hidden_core = swap(hidden, "rows", 1)
    while bit > 2:
        bit //= 2
        earlier = jnp.concatenate([gathered, received])
        received = swap(earlier, "tm", bit)
        gathered = earlier
    beside = swap(gathered, "tm", 1)
    state = attend([hidden, hidden_core], wk, wv, query)
    state, received, beside, hidden_y = lax.optimization_barrier((state, received, beside, hidden_y))
    beside_late = swap(received, "tm", 1)
    ref_early = jnp.concatenate([gathered, received, beside])
    ref_early_core = swap(ref_early, "rows", 1)
    hidden_far = swap(hidden_y, "rows", 1)
    state = attend([ref_early, ref_early_core], wk, wv, query, state)
    state, beside_late = lax.optimization_barrier((state, beside_late))
    ref_late_core = swap(beside_late, "rows", 1)
    attended = attend(
        [hidden_y, hidden_far, beside_late, ref_late_core],
        wk,
        wv,
        query,
        state,
        (wo, out_bias),
    )
    return (
        hidden_final.reshape(count, band_rows, width, channels),
        attended.reshape(count, band_rows, width, channels),
    )


def solution(mesh):
    return jax.shard_map(
        shards,
        mesh=mesh,
        in_specs=(P("tm", "rows", None, None), P(), P(), P("tm", None), P(), P(), P(), P(), P()),
        out_specs=(P("tm", "rows", None, None), P("tm", "rows", None, None)),
        check_vma=False,
    )
```

```python
import functools

import jax
import jax.numpy as jnp
from jax import lax
from jax.experimental import pallas as pl
from jax.experimental.pallas import tpu as pltpu
from jax.sharding import PartitionSpec as P

HD = 80
LANES = 128
SCALE = HD ** (-0.5) * 1.4426950408889634
BF = jnp.bfloat16
F32 = jnp.float32
VMEM_LIMIT = 24 << 20
LONG = pl.CostEstimate(flops=20 << 30, bytes_accessed=32 << 20, transcendentals=0)
COST = pl.CostEstimate(flops=1 << 10, bytes_accessed=1 << 10, transcendentals=0)


def vmem_call(body, outs, scratch, *operands):
    whole = pl.BlockSpec(memory_space=pltpu.VMEM)
    return pl.pallas_call(
        body,
        out_shape=outs,
        in_specs=[whole] * len(operands),
        out_specs=jax.tree.map(lambda _: whole, outs),
        scratch_shapes=scratch,
        cost_estimate=COST,
        compiler_params=pltpu.CompilerParams(vmem_limit_bytes=VMEM_LIMIT),
    )(*operands)


def silu(value):
    value = value.astype(F32)
    return value / (1.0 + jnp.exp(-value))


def shift_columns(active, width):
    rows = active.shape[0]
    column = lax.broadcasted_iota(jnp.int32, active.shape, 0) % width
    left = jnp.where(column == 0, 0.0, pltpu.roll(active, 1, 0))
    right = jnp.where(column == width - 1, 0.0, pltpu.roll(active, rows - 1, 0))
    return left.astype(BF), active.astype(BF), right.astype(BF)


def sending_kernel(
    core, x_in, ref_in, core_out, cross_out, ref_out, rows, ref, row_sem, ref_sem
):
    width = core_out.shape[0]
    band = x_in.shape[0]
    half = ref_out.shape[0]
    copies = [
        pltpu.make_async_copy(x_in.at[:width], rows.at[0], row_sem.at[0]),
        pltpu.make_async_copy(x_in.at[band - width :], rows.at[1], row_sem.at[1]),
        pltpu.make_async_copy(ref_in, ref, ref_sem),
    ]
    for copy in copies:
        copy.start()
    for copy in copies:
        copy.wait()
    is_first = core[0] == 0
    first, last = rows[0], rows[1]
    core_out[...] = jnp.where(is_first, last, first)
    cross_out[...] = jnp.where(is_first, first, last)
    whole = ref[...]
    ref_out[...] = jnp.where(is_first, whole[:half], whole[half:])


def sending(core, x, ref, width):
    band, channels = x.shape
    shape = jax.ShapeDtypeStruct
    near = pl.BlockSpec(memory_space=pltpu.VMEM)
    return pl.pallas_call(
        sending_kernel,
        out_shape=(
            shape((width, channels), BF),
            shape((width, channels), BF),
            shape((ref.shape[0] // 2, channels), BF),
        ),
        in_specs=[pl.BlockSpec(memory_space=pltpu.SMEM)]
        + [pl.BlockSpec(memory_space=pltpu.HBM)] * 2,
        out_specs=(near,) * 3,
        scratch_shapes=[
            pltpu.VMEM((2, width, channels), BF),
            pltpu.VMEM(ref.shape, BF),
            pltpu.SemaphoreType.DMA((2,)),
            pltpu.SemaphoreType.DMA,
        ],
        cost_estimate=LONG,
        compiler_params=pltpu.CompilerParams(vmem_limit_bytes=4 << 20),
    )(core, *[pltpu.with_memory_space_constraint(v, pltpu.HBM) for v in (x, ref)])


def opening_kernel(width, x, weight, bias, wk, wv, wo, total_out, wk_out, wv_out, wo_out, shifted):
    band, channels = x.shape
    heads = channels // HD
    for col, part in enumerate(shift_columns(silu(x[...]), width)):
        shifted[col] = part
    wk_out[...] = wk[...].T
    wv_out[...] = wv[...].T
    wo_out[...] = jnp.zeros_like(wo_out)
    for head in range(heads):
        wo_out[head * LANES : head * LANES + HD, :] = wo[head * HD : (head + 1) * HD, :]
    total = x[...].astype(F32) + bias[...][None, :]
    for col in range(3):
        total = total + jnp.dot(shifted[col], weight[1, col], preferred_element_type=F32)
    total_out[...] = total
    for row, source, target in (
        (0, slice(0, band - width), slice(width, band)),
        (2, slice(width, band), slice(0, band - width)),
    ):
        part = total_out[target]
        for col in range(3):
            part = part + jnp.dot(
                shifted[col, source], weight[row, col], preferred_element_type=F32
            )
        total_out[target] = part


def opening(x, weight, bias, wk, wv, wo, width):
    band, channels = x.shape
    heads = channels // HD
    shape = jax.ShapeDtypeStruct
    square = shape((channels, channels), BF)
    return vmem_call(
        functools.partial(opening_kernel, width),
        (shape((band, channels), F32), square, square, shape((heads * LANES, channels), BF)),
        [pltpu.VMEM((3, band, channels), BF)],
        x,
        weight,
        bias,
        wk,
        wv,
        wo,
    )


def conv_kernel(
    width, core, core_row, cross_row, total, weight, wq, hidden_out, query_out
):
    band, channels = total.shape
    heads = channels // HD
    query_out[...] = jnp.zeros_like(query_out)
    is_first = core[0] == 0
    core_part, cross_part = core_row[...], cross_row[...]
    above = shift_columns(silu(jnp.where(is_first, cross_part, core_part)), width)
    below = shift_columns(silu(jnp.where(is_first, core_part, cross_part)), width)
    top, bottom = total[:width], total[band - width :]
    for col in range(3):
        top = top + jnp.dot(above[col], weight[0, col], preferred_element_type=F32)
        bottom = bottom + jnp.dot(below[col], weight[2, col], preferred_element_type=F32)
    hidden_out[width : band - width] = total[width : band - width].astype(BF)
    hidden_out[:width] = top.astype(BF)
    hidden_out[band - width :] = bottom.astype(BF)
    query = (
        jnp.dot(hidden_out[...], wq[...], preferred_element_type=F32) * SCALE
    ).astype(BF)
    for head in range(heads):
        query_out[:, head * LANES : head * LANES + HD] = query[:, head * HD : (head + 1) * HD]


def conv(core, core_row, cross_row, total, weight, wq, width):
    band, channels = total.shape
    heads = channels // HD
    shape = jax.ShapeDtypeStruct
    near = pl.BlockSpec(memory_space=pltpu.VMEM)
    return pl.pallas_call(
        functools.partial(conv_kernel, width),
        out_shape=(shape((band, channels), BF), shape((band, heads * LANES), BF)),
        in_specs=[pl.BlockSpec(memory_space=pltpu.SMEM)] + [near] * 5,
        out_specs=(near,) * 2,
        cost_estimate=COST,
        compiler_params=pltpu.CompilerParams(vmem_limit_bytes=VMEM_LIMIT),
    )(core, core_row, cross_row, total, weight, wq)


def attend_kernel(pieces, first, last, *refs):
    refs = list(refs)
    sources = [refs.pop(0) for _ in range(pieces)]
    wk, wv, query = [refs.pop(0) for _ in range(3)]
    if not first:
        top_in, sum_in = refs.pop(0), refs.pop(0)
    if last:
        wo, bias, hidden, out, hidden_out, keys, values, mixed = refs
    else:
        top_out, sum_out, keys, values = refs
    channels = wk.shape[0]
    heads = channels // HD
    band = query.shape[0]
    tokens = keys.shape[1]
    keys[channels:, :] = jnp.zeros((keys.shape[0] - channels, tokens), BF)
    start = 0
    for source in sources:
        part = source[...]
        length = part.shape[0]
        here = slice(start, start + length)
        contract = (((1,), (1,)), ((), ()))
        keys[:channels, here] = lax.dot_general(
            wk[...], part, contract, preferred_element_type=F32
        ).astype(BF)
        value = lax.dot_general(wv[...], part, contract, preferred_element_type=F32).astype(BF)
        for head in range(heads):
            values[head * LANES : head * LANES + HD, here] = value[head * HD : (head + 1) * HD]
            values[head * LANES + HD : (head + 1) * LANES, here] = jnp.ones(
                (LANES - HD, length), BF
            )
        start += length

    def score(head):
        return jnp.dot(
            query[:, head * LANES : (head + 1) * LANES],
            keys[head * HD : head * HD + LANES, :],
            preferred_element_type=F32,
        )

    def weigh(scores, head):
        top = jnp.broadcast_to(jnp.max(scores, axis=1, keepdims=True), (band, LANES))
        if not first:
            top = jnp.maximum(top, top_in[head])
        weights = jnp.concatenate(
            [
                jnp.exp2(scores[:, at : at + LANES] - top).astype(BF)
                for at in range(0, tokens, LANES)
            ],
            axis=1,
        )
        return top, weights

    def finish(head, top, weights):
        product = lax.dot_general(
            weights,
            values[head * LANES : (head + 1) * LANES, :],
            (((1,), (1,)), ((), ())),
            preferred_element_type=F32,
        )
        if not first:
            product = product + sum_in[head] * jnp.exp2(top_in[head] - top)
        if last:
            mixed[:, head * LANES : (head + 1) * LANES] = (
                product / product[:, HD : HD + 1]
            ).astype(BF)
        else:
            top_out[head] = top
            sum_out[head] = product

    scores, ready = score(0), None
    for head in range(heads + 1):
        upcoming = score(head + 1) if head + 1 < heads else None
        weighed = weigh(scores, head) if head < heads else None
        if ready is not None:
            finish(head - 1, *ready)
        scores, ready = upcoming, weighed
    if last:
        hidden_out[...] = hidden[...]
        out[...] = (
            jnp.dot(mixed[...], wo[...], preferred_element_type=F32) + bias[...][None, :]
        ).astype(BF)


def attend(sources, wk, wv, query, state=None, final=None):
    channels = wk.shape[0]
    heads = channels // HD
    band = query.shape[0]
    tokens = sum(source.shape[0] for source in sources)
    shape = jax.ShapeDtypeStruct
    scratch = [
        pltpu.VMEM((channels - HD + LANES, tokens), BF),
        pltpu.VMEM((heads * LANES, tokens), BF),
    ]
    operands = list(sources) + [wk, wv, query]
    if state is not None:
        operands += list(state)
    if final is not None:
        operands += list(final)
        outs = (shape((band, channels), BF), shape((band, channels), BF))
        scratch.append(pltpu.VMEM((band, heads * LANES), BF))
    else:
        outs = (shape((heads, band, LANES), F32), shape((heads, band, LANES), F32))
    return vmem_call(
        functools.partial(attend_kernel, len(sources), state is None, final is not None),
        outs,
        scratch,
        *operands,
    )


def swap(value, axis, bit):
    size = lax.axis_size(axis)
    return lax.ppermute(value, axis, [(i, i ^ bit) for i in range(size)])


def shards(frames, conv_weight, conv_bias, ref_features, w_query, w_key, w_value, w_out, out_bias):
    count, band_rows, width, channels = frames.shape
    band = band_rows * width
    x = frames.reshape(count * band, channels)
    core = (lax.axis_index("rows") % 2).reshape(1).astype(jnp.int32)
    core_row, cross_row, gathered = sending(core, x, ref_features, width)
    between = [(i, i + 1) for i in range(1, lax.axis_size("rows") - 1, 2)]
    cross_row = lax.ppermute(cross_row, "rows", between + [(j, i) for i, j in between])
    core_row = swap(core_row, "rows", 1)
    bit = lax.axis_size("tm") // 2
    while bit > 4:
        gathered = jnp.concatenate([gathered, swap(gathered, "tm", bit)])
        bit //= 2
    beside = swap(gathered, "tm", 1)
    column = [swap(gathered, "tm", part) for part in (4, 2, 6)]
    total, wk, wv, wo = opening(
        x, conv_weight, conv_bias, w_key, w_value, w_out, width
    )
    hidden, query = conv(core, core_row, cross_row, total, conv_weight, w_query, width)
    column, beside, hidden = lax.optimization_barrier((column, beside, hidden))
    others = jnp.concatenate(column)
    column = jnp.concatenate([gathered, others])
    column_core = swap(column, "rows", 1)
    hidden_core = swap(hidden, "rows", 1)
    others = swap(others, "tm", 1)
    hidden_y = swap(hidden, "rows", 2)
    state = attend([hidden, hidden_core, column, column_core], wk, wv, query)
    state, hidden_y, others = lax.optimization_barrier((state, hidden_y, others))
    beside = jnp.concatenate([beside, others])
    hidden_far = swap(hidden_y, "rows", 1)
    beside_core = swap(beside, "rows", 1)
    state = attend([hidden_y, beside], wk, wv, query, state)
    attended, hidden = attend(
        [hidden_far, beside_core], wk, wv, query, state, (wo, out_bias, hidden)
    )
    return (
        hidden.reshape(count, band_rows, width, channels),
        attended.reshape(count, band_rows, width, channels),
    )


def solution(mesh):
    return jax.shard_map(
        shards,
        mesh=mesh,
        in_specs=(P("tm", "rows", None, None), P(), P(), P("tm", None), P(), P(), P(), P(), P()),
        out_specs=(P("tm", "rows", None, None), P("tm", "rows", None, None)),
        check_vma=False,
    )
```

```python
import functools

import jax
import jax.numpy as jnp
from jax import lax
from jax.experimental import pallas as pl
from jax.experimental.pallas import tpu as pltpu
from jax.sharding import PartitionSpec as P

HD = 80
LANES = 128
SCALE = HD ** (-0.5) * 1.4426950408889634
BF = jnp.bfloat16
F32 = jnp.float32
VMEM_LIMIT = 24 << 20
LONG = pl.CostEstimate(flops=20 << 30, bytes_accessed=32 << 20, transcendentals=0)
COST = pl.CostEstimate(flops=1 << 10, bytes_accessed=1 << 10, transcendentals=0)


def vmem_call(body, outs, scratch, *operands, place=pltpu.VMEM):
    whole = pl.BlockSpec(memory_space=pltpu.VMEM)
    return pl.pallas_call(
        body,
        out_shape=outs,
        in_specs=[whole] * len(operands),
        out_specs=jax.tree.map(lambda _: pl.BlockSpec(memory_space=place), outs),
        scratch_shapes=scratch,
        cost_estimate=COST,
        compiler_params=pltpu.CompilerParams(vmem_limit_bytes=VMEM_LIMIT),
    )(*operands)


def silu(value):
    value = value.astype(F32)
    return value / (1.0 + jnp.exp(-value))


def shift_columns(active, width):
    rows = active.shape[0]
    column = lax.broadcasted_iota(jnp.int32, active.shape, 0) % width
    left = jnp.where(column == 0, 0.0, pltpu.roll(active, 1, 0))
    right = jnp.where(column == width - 1, 0.0, pltpu.roll(active, rows - 1, 0))
    return left.astype(BF), active.astype(BF), right.astype(BF)


def place():
    row = lax.axis_index("rows")
    return row % 2 == 0, (row > 0) & (row < lax.axis_size("rows") - 1)


def sending_kernel(
    x_in, ref_in, core_out, first_out, own_out, half_out, rows, row_sem, ref_sem
):
    width = core_out.shape[0]
    band = x_in.shape[0]
    copies = [
        pltpu.make_async_copy(x_in.at[:width], rows.at[0], row_sem.at[0]),
        pltpu.make_async_copy(x_in.at[band - width :], rows.at[1], row_sem.at[1]),
        pltpu.make_async_copy(ref_in, own_out, ref_sem),
    ]
    for copy in copies:
        copy.start()
    for copy in copies:
        copy.wait()
    is_first, is_inner = place()
    first, last = rows[0], rows[1]
    core_out[...] = jnp.where(is_first, last, first)
    own = own_out[...]
    half = half_out.shape[0]
    half_out[...] = jnp.where(is_first, own[:half], own[half:])
    first_out[...] = own
    first_out[:width] = jnp.where(is_inner, jnp.where(is_first, first, last), own[:width])


def sending(x, ref, width):
    channels = x.shape[1]
    shape = jax.ShapeDtypeStruct
    near = pl.BlockSpec(memory_space=pltpu.VMEM)
    far = pl.BlockSpec(memory_space=pltpu.HBM)
    return pl.pallas_call(
        sending_kernel,
        out_shape=(
            shape((width, channels), BF),
            shape(ref.shape, BF),
            shape(ref.shape, BF),
            shape((ref.shape[0] // 2, channels), BF),
        ),
        in_specs=[far, far],
        out_specs=(near,) * 4,
        scratch_shapes=[
            pltpu.VMEM((2, width, channels), BF),
            pltpu.SemaphoreType.DMA((2,)),
            pltpu.SemaphoreType.DMA,
        ],
        cost_estimate=LONG,
        compiler_params=pltpu.CompilerParams(vmem_limit_bytes=4 << 20),
    )(*[pltpu.with_memory_space_constraint(v, pltpu.HBM) for v in (x, ref)])


def opening_kernel(width, x, weight, bias, total_out, shifted):
    band, channels = x.shape
    for col, part in enumerate(shift_columns(silu(x[...]), width)):
        shifted[col] = part
    total = x[...].astype(F32) + bias[...][None, :]
    for col in range(3):
        total = total + jnp.dot(shifted[col], weight[1, col], preferred_element_type=F32)
    total_out[...] = total
    for row, source, target in (
        (0, slice(0, band - width), slice(width, band)),
        (2, slice(width, band), slice(0, band - width)),
    ):
        part = total_out[target]
        for col in range(3):
            part = part + jnp.dot(
                shifted[col, source], weight[row, col], preferred_element_type=F32
            )
        total_out[target] = part


def opening(x, weight, bias, width):
    band, channels = x.shape
    return vmem_call(
        functools.partial(opening_kernel, width),
        jax.ShapeDtypeStruct((band, channels), F32),
        [pltpu.VMEM((3, band, channels), BF)],
        x,
        weight,
        bias,
    )


def conv_kernel(
    width, core_row, cross_row, total, weight, hidden_out
):
    band, channels = total.shape
    is_first, is_inner = place()
    core_part = core_row[...]
    cross_part = jnp.where(is_inner, cross_row[:width], jnp.zeros_like(core_part))
    above = shift_columns(silu(jnp.where(is_first, cross_part, core_part)), width)
    below = shift_columns(silu(jnp.where(is_first, core_part, cross_part)), width)
    top, bottom = total[:width], total[band - width :]
    for col in range(3):
        top = top + jnp.dot(above[col], weight[0, col], preferred_element_type=F32)
        bottom = bottom + jnp.dot(below[col], weight[2, col], preferred_element_type=F32)
    hidden_out[width : band - width] = total[width : band - width].astype(BF)
    hidden_out[:width] = top.astype(BF)
    hidden_out[band - width :] = bottom.astype(BF)


def conv(core_row, cross_row, total, weight, width):
    near = pl.BlockSpec(memory_space=pltpu.VMEM)
    return pl.pallas_call(
        functools.partial(conv_kernel, width),
        out_shape=jax.ShapeDtypeStruct(total.shape, BF),
        in_specs=[near] * 4,
        out_specs=near,
        cost_estimate=COST,
        compiler_params=pltpu.CompilerParams(vmem_limit_bytes=VMEM_LIMIT),
    )(core_row, cross_row, total, weight)


def pairing_kernel(first, far_half, own, pair):
    _, is_inner = place()
    block = own.shape[0]
    pair[:block] = jnp.where(is_inner, own[...], first[...])
    pair[block:] = far_half[...]


def pairing(first, far_half, own):
    rows = own.shape[0] + far_half.shape[0]
    shape = jax.ShapeDtypeStruct((rows, own.shape[1]), BF)
    return vmem_call(pairing_kernel, shape, [], first, far_half, own)


def attend_kernel(pieces, first, last, *refs):
    refs = list(refs)
    sources = [refs.pop(0) for _ in range(pieces)]
    wk, wv, query = [refs.pop(0) for _ in range(3)]
    channels = wk.shape[0]
    heads = channels // HD
    if first:
        top_out, sum_out, wk_out, wv_out, query_out, keys, values, column = refs
        own, pair, pair_core = sources[2:]
        _, is_inner = place()
        block = own.shape[0]
        column[:block] = own[...]
        column[block : 2 * block] = jnp.where(is_inner, pair_core[:block], pair[:block])
        middle = 2 * block + pair.shape[0] - block
        column[2 * block : middle] = pair[block:]
        column[middle:] = pair_core[block:]
        sources = sources[:2] + [column]
        wk_out[...] = wk[...].T
        wv_out[...] = wv[...].T
        projected = (
            jnp.dot(sources[0][...], query[...], preferred_element_type=F32) * SCALE
        ).astype(BF)
        query_out[...] = jnp.zeros_like(query_out)
        for head in range(heads):
            query_out[:, head * LANES : head * LANES + HD] = projected[
                :, head * HD : (head + 1) * HD
            ]
        wk, wv, query = wk_out, wv_out, query_out
    else:
        top_in, sum_in = refs.pop(0), refs.pop(0)
        if last:
            wo, bias, hidden, out, hidden_out, keys, values, mixed, out_work, out_sem, hidden_sem = refs
            hidden_copy = pltpu.make_async_copy(hidden, hidden_out, hidden_sem)
            hidden_copy.start()
            mixed[...] = jnp.zeros_like(mixed)
        else:
            top_out, sum_out, keys, values = refs
    band = query.shape[0]
    tokens = keys.shape[1]
    keys[channels:, :] = jnp.zeros((keys.shape[0] - channels, tokens), BF)
    start = 0
    for source in sources:
        part = source[...]
        length = part.shape[0]
        here = slice(start, start + length)
        contract = (((1,), (1,)), ((), ()))
        keys[:channels, here] = lax.dot_general(
            wk[...], part, contract, preferred_element_type=F32
        ).astype(BF)
        value = lax.dot_general(wv[...], part, contract, preferred_element_type=F32).astype(BF)
        for head in range(heads):
            values[head * LANES : head * LANES + HD, here] = value[head * HD : (head + 1) * HD]
            values[head * LANES + HD : (head + 1) * LANES, here] = jnp.ones(
                (LANES - HD, length), BF
            )
        start += length

    def score(head):
        return jnp.dot(
            query[:, head * LANES : (head + 1) * LANES],
            keys[head * HD : head * HD + LANES, :],
            preferred_element_type=F32,
        )

    def weigh(scores, head):
        top = jnp.broadcast_to(jnp.max(scores, axis=1, keepdims=True), (band, LANES))
        if not first:
            top = jnp.maximum(top, top_in[head])
        weights = jnp.concatenate(
            [
                jnp.exp2(scores[:, at : at + LANES] - top).astype(BF)
                for at in range(0, tokens, LANES)
            ],
            axis=1,
        )
        return top, weights

    def finish(head, top, weights):
        product = lax.dot_general(
            weights,
            values[head * LANES : (head + 1) * LANES, :],
            (((1,), (1,)), ((), ())),
            preferred_element_type=F32,
        )
        if not first:
            product = product + sum_in[head] * jnp.exp2(top_in[head] - top)
        if last:
            mixed[:, head * HD : (head + 1) * HD] = (
                product[:, :HD] / product[:, HD : HD + 1]
            ).astype(BF)
        else:
            top_out[head] = top
            sum_out[head] = product

    scores, ready = score(0), None
    for head in range(heads + 1):
        upcoming = score(head + 1) if head + 1 < heads else None
        weighed = weigh(scores, head) if head < heads else None
        if ready is not None:
            finish(head - 1, *ready)
        scores, ready = upcoming, weighed
    if last:
        copies = []
        for i in range(2):
            here = slice(i * band // 2, (i + 1) * band // 2)
            out_work[here, :] = (
                jnp.dot(mixed[here, :], wo[...], preferred_element_type=F32) + bias[...][None, :]
            ).astype(BF)
            copies.append(pltpu.make_async_copy(out_work.at[here], out.at[here], out_sem.at[i]))
            copies[-1].start()
        for copy in copies + [hidden_copy]:
            copy.wait()


def attend(sources, wk, wv, query, state=None, final=None):
    channels = wk.shape[0]
    heads = channels // HD
    band = sources[0].shape[0] if state is None else query.shape[0]
    tokens = sum(source.shape[0] for source in sources)
    if state is None:
        tokens -= sources[2].shape[0]
    shape = jax.ShapeDtypeStruct
    carried = shape((heads, band, LANES), F32)
    square = shape((channels, channels), BF)
    scratch = [
        pltpu.VMEM((channels - HD + LANES, tokens), BF),
        pltpu.VMEM((heads * LANES, tokens), BF),
    ]
    operands = list(sources) + [wk, wv, query] + list(state or ()) + list(final or ())
    place = pltpu.VMEM
    if final is not None:
        outs = (shape((band, channels), BF), shape((band, channels), BF))
        scratch += [
            pltpu.VMEM((band, channels), BF),
            pltpu.VMEM((band, channels), BF),
            pltpu.SemaphoreType.DMA((2,)),
            pltpu.SemaphoreType.DMA,
        ]
        place = pltpu.HBM
    elif state is None:
        scratch.append(pltpu.VMEM((tokens - 2 * band, channels), BF))
        outs = (carried, carried, square, square, shape((band, heads * LANES), BF))
    else:
        outs = (carried, carried)
    return vmem_call(
        functools.partial(attend_kernel, len(sources), state is None, final is not None),
        outs,
        scratch,
        *operands,
        place=place,
    )


def swap(value, axis, bit):
    size = lax.axis_size(axis)
    return lax.ppermute(value, axis, [(i, i ^ bit) for i in range(size)])


def shards(frames, conv_weight, conv_bias, ref_features, w_query, w_key, w_value, w_out, out_bias):
    count, band_rows, width, channels = frames.shape
    band = band_rows * width
    x = frames.reshape(count * band, channels)
    tm, rows = lax.axis_size("tm"), lax.axis_size("rows")
    own = ref_features
    bit = tm // 2
    while bit > 4:
        own = jnp.concatenate([own, swap(own, "tm", bit)])
        bit //= 2
    core_row, first, own, far_half = sending(x, own, width)
    inner = range(1, rows - 1)
    partner = {i: i + 1 if i % 2 else i - 1 for i in inner}
    everyone = [(t, r) for t in range(tm) for r in range(rows)]
    far_half = swap(far_half, "tm", 4)
    first = lax.ppermute(
        first,
        ("tm", "rows"),
        [
            (t * rows + r, t * rows + partner[r] if r in partner else (t ^ 2) * rows + r)
            for t, r in everyone
        ],
    )
    core_row = swap(core_row, "rows", 1)
    total = opening(x, conv_weight, conv_bias, width)
    hidden = conv(core_row, first, total, conv_weight, width)
    pair = pairing(first, far_half, own)
    pair_core = swap(pair, "rows", 1)
    hidden_core = swap(hidden, "rows", 1)
    corner_half = swap(far_half, "tm", 2)
    last_half = swap(far_half, "tm", 3)
    beside = swap(pair, "tm", 1)
    hidden_y = swap(hidden, "rows", 2)
    *state, wk, wv, query = attend(
        [hidden, hidden_core, own, pair, pair_core], w_key, w_value, w_query
    )
    state, hidden_y, beside, corner_half, last_half = lax.optimization_barrier(
        (state, hidden_y, beside, corner_half, last_half)
    )
    across = jnp.concatenate([beside, corner_half])
    hidden_far = swap(hidden_y, "rows", 1)
    across_core = swap(jnp.concatenate([across, last_half]), "rows", 1)
    state = attend([hidden_y, across], wk, wv, query, state)
    attended, hidden = attend(
        [hidden_far, jnp.concatenate([across_core, last_half])],
        wk,
        wv,
        query,
        state,
        (w_out, out_bias, hidden),
    )
    return (
        hidden.reshape(count, band_rows, width, channels),
        attended.reshape(count, band_rows, width, channels),
    )


def solution(mesh):
    return jax.shard_map(
        shards,
        mesh=mesh,
        in_specs=(P("tm", "rows", None, None), P(), P(), P("tm", None), P(), P(), P(), P(), P()),
        out_specs=(P("tm", "rows", None, None), P("tm", "rows", None, None)),
        check_vma=False,
    )
```

```python
import functools

import jax
import jax.numpy as jnp
from jax import lax
from jax.experimental import pallas as pl
from jax.experimental.pallas import tpu as pltpu
from jax.sharding import PartitionSpec as P

HD = 80
LANES = 128
SCALE = HD ** (-0.5) * 1.4426950408889634
BF = jnp.bfloat16
F32 = jnp.float32
VMEM_LIMIT = 24 << 20
LONG = pl.CostEstimate(flops=20 << 30, bytes_accessed=32 << 20, transcendentals=0)
COST = pl.CostEstimate(flops=1 << 10, bytes_accessed=1 << 10, transcendentals=0)


def vmem_call(body, outs, scratch, *operands, place=pltpu.VMEM):
    whole = pl.BlockSpec(memory_space=pltpu.VMEM)
    return pl.pallas_call(
        body,
        out_shape=outs,
        in_specs=[whole] * len(operands),
        out_specs=jax.tree.map(lambda _: pl.BlockSpec(memory_space=place), outs),
        scratch_shapes=scratch,
        cost_estimate=COST,
        compiler_params=pltpu.CompilerParams(vmem_limit_bytes=VMEM_LIMIT),
    )(*operands)


def silu(value):
    value = value.astype(F32)
    return value / (1.0 + jnp.exp(-value))


def shift_columns(active, width):
    rows = active.shape[0]
    column = lax.broadcasted_iota(jnp.int32, active.shape, 0) % width
    left = jnp.where(column == 0, 0.0, pltpu.roll(active, 1, 0))
    right = jnp.where(column == width - 1, 0.0, pltpu.roll(active, rows - 1, 0))
    return left.astype(BF), active.astype(BF), right.astype(BF)


def place():
    row = lax.axis_index("rows")
    return row % 2 == 0, (row > 0) & (row < lax.axis_size("rows") - 1)


def sending_kernel(
    x_in, ref_in, core_out, first_out, own_out, half_out, rows, row_sem, ref_sem
):
    width = core_out.shape[0]
    band = x_in.shape[0]
    copies = [
        pltpu.make_async_copy(x_in.at[:width], rows.at[0], row_sem.at[0]),
        pltpu.make_async_copy(x_in.at[band - width :], rows.at[1], row_sem.at[1]),
        pltpu.make_async_copy(ref_in, own_out, ref_sem),
    ]
    for copy in copies:
        copy.start()
    for copy in copies:
        copy.wait()
    is_first, is_inner = place()
    first, last = rows[0], rows[1]
    core_out[...] = jnp.where(is_first, last, first)
    own = own_out[...]
    half = half_out.shape[0]
    half_out[...] = jnp.where(is_first, own[:half], own[half:])
    first_out[...] = own
    first_out[:width] = jnp.where(is_inner, jnp.where(is_first, first, last), own[:width])


def sending(x, ref, width):
    channels = x.shape[1]
    shape = jax.ShapeDtypeStruct
    near = pl.BlockSpec(memory_space=pltpu.VMEM)
    far = pl.BlockSpec(memory_space=pltpu.HBM)
    return pl.pallas_call(
        sending_kernel,
        out_shape=(
            shape((width, channels), BF),
            shape(ref.shape, BF),
            shape(ref.shape, BF),
            shape((ref.shape[0] // 2, channels), BF),
        ),
        in_specs=[far, far],
        out_specs=(near,) * 4,
        scratch_shapes=[
            pltpu.VMEM((2, width, channels), BF),
            pltpu.SemaphoreType.DMA((2,)),
            pltpu.SemaphoreType.DMA,
        ],
        cost_estimate=LONG,
        compiler_params=pltpu.CompilerParams(vmem_limit_bytes=4 << 20),
    )(*[pltpu.with_memory_space_constraint(v, pltpu.HBM) for v in (x, ref)])


def opening_kernel(width, x, weight, bias, total_out, shifted):
    band, channels = x.shape
    for col, part in enumerate(shift_columns(silu(x[...]), width)):
        shifted[col] = part
    total = x[...].astype(F32) + bias[...][None, :]
    for col in range(3):
        total = total + jnp.dot(shifted[col], weight[1, col], preferred_element_type=F32)
    total_out[...] = total
    for row, source, target in (
        (0, slice(0, band - width), slice(width, band)),
        (2, slice(width, band), slice(0, band - width)),
    ):
        part = total_out[target]
        for col in range(3):
            part = part + jnp.dot(
                shifted[col, source], weight[row, col], preferred_element_type=F32
            )
        total_out[target] = part


def opening(x, weight, bias, width):
    band, channels = x.shape
    return vmem_call(
        functools.partial(opening_kernel, width),
        jax.ShapeDtypeStruct((band, channels), F32),
        [pltpu.VMEM((3, band, channels), BF)],
        x,
        weight,
        bias,
    )


def conv_kernel(
    width, core_row, cross_row, total, weight, hidden_out
):
    band, channels = total.shape
    is_first, is_inner = place()
    core_part = core_row[...]
    cross_part = jnp.where(is_inner, cross_row[:width], jnp.zeros_like(core_part))
    above = shift_columns(silu(jnp.where(is_first, cross_part, core_part)), width)
    below = shift_columns(silu(jnp.where(is_first, core_part, cross_part)), width)
    top, bottom = total[:width], total[band - width :]
    for col in range(3):
        top = top + jnp.dot(above[col], weight[0, col], preferred_element_type=F32)
        bottom = bottom + jnp.dot(below[col], weight[2, col], preferred_element_type=F32)
    hidden_out[width : band - width] = total[width : band - width].astype(BF)
    hidden_out[:width] = top.astype(BF)
    hidden_out[band - width :] = bottom.astype(BF)


def conv(core_row, cross_row, total, weight, width):
    near = pl.BlockSpec(memory_space=pltpu.VMEM)
    return pl.pallas_call(
        functools.partial(conv_kernel, width),
        out_shape=jax.ShapeDtypeStruct(total.shape, BF),
        in_specs=[near] * 4,
        out_specs=near,
        cost_estimate=COST,
        compiler_params=pltpu.CompilerParams(vmem_limit_bytes=VMEM_LIMIT),
    )(core_row, cross_row, total, weight)


def pairing_kernel(first, far_half, own, pair):
    _, is_inner = place()
    block = own.shape[0]
    pair[:block] = jnp.where(is_inner, own[...], first[...])
    pair[block:] = far_half[...]


def pairing(first, far_half, own):
    rows = own.shape[0] + far_half.shape[0]
    shape = jax.ShapeDtypeStruct((rows, own.shape[1]), BF)
    return vmem_call(pairing_kernel, shape, [], first, far_half, own)


def attend_kernel(pieces, first, last, *refs):
    refs = list(refs)
    sources = [refs.pop(0) for _ in range(pieces)]
    wk, wv, query = [refs.pop(0) for _ in range(3)]
    channels = wk.shape[0]
    heads = channels // HD
    if first:
        wo, top_out, sum_out, wk_out, wv_out, query_out, wo_out, keys, values, column = refs
        wo_out[...] = jnp.zeros_like(wo_out)
        for head in range(heads):
            wo_out[head * LANES : head * LANES + HD, :] = wo[head * HD : (head + 1) * HD, :]
        own, pair, pair_core = sources[2:]
        _, is_inner = place()
        block = own.shape[0]
        column[:block] = own[...]
        column[block : 2 * block] = jnp.where(is_inner, pair_core[:block], pair[:block])
        middle = 2 * block + pair.shape[0] - block
        column[2 * block : middle] = pair[block:]
        column[middle:] = pair_core[block:]
        sources = sources[:2] + [column]
        wk_out[...] = wk[...].T
        wv_out[...] = wv[...].T
        projected = (
            jnp.dot(sources[0][...], query[...], preferred_element_type=F32) * SCALE
        ).astype(BF)
        query_out[...] = jnp.zeros_like(query_out)
        for head in range(heads):
            query_out[:, head * LANES : head * LANES + HD] = projected[
                :, head * HD : (head + 1) * HD
            ]
        wk, wv, query = wk_out, wv_out, query_out
    else:
        top_in, sum_in = refs.pop(0), refs.pop(0)
        if last:
            wo, bias, hidden, out, hidden_out, keys, values, mixed, out_work, out_sem, hidden_sem = refs
            hidden_copy = pltpu.make_async_copy(hidden, hidden_out, hidden_sem)
            hidden_copy.start()
        else:
            top_out, sum_out, keys, values = refs
    band = query.shape[0]
    tokens = keys.shape[1]
    keys[channels:, :] = jnp.zeros((keys.shape[0] - channels, tokens), BF)
    start = 0
    for source in sources:
        part = source[...]
        length = part.shape[0]
        here = slice(start, start + length)
        contract = (((1,), (1,)), ((), ()))
        keys[:channels, here] = lax.dot_general(
            wk[...], part, contract, preferred_element_type=F32
        ).astype(BF)
        value = lax.dot_general(wv[...], part, contract, preferred_element_type=F32).astype(BF)
        for head in range(heads):
            values[head * LANES : head * LANES + HD, here] = value[head * HD : (head + 1) * HD]
            values[head * LANES + HD : (head + 1) * LANES, here] = jnp.ones(
                (LANES - HD, length), BF
            )
        start += length

    def score(head):
        return jnp.dot(
            query[:, head * LANES : (head + 1) * LANES],
            keys[head * HD : head * HD + LANES, :],
            preferred_element_type=F32,
        )

    def weigh(scores, head):
        top = jnp.broadcast_to(jnp.max(scores, axis=1, keepdims=True), (band, LANES))
        if not first:
            top = jnp.maximum(top, top_in[head])
        weights = jnp.concatenate(
            [
                jnp.exp2(scores[:, at : at + LANES] - top).astype(BF)
                for at in range(0, tokens, LANES)
            ],
            axis=1,
        )
        return top, weights

    def finish(head, top, weights):
        product = lax.dot_general(
            weights,
            values[head * LANES : (head + 1) * LANES, :],
            (((1,), (1,)), ((), ())),
            preferred_element_type=F32,
        )
        if not first:
            product = product + sum_in[head] * jnp.exp2(top_in[head] - top)
        if last:
            mixed[:, head * LANES : (head + 1) * LANES] = (
                product / product[:, HD : HD + 1]
            ).astype(BF)
        else:
            top_out[head] = top
            sum_out[head] = product

    scores, ready = score(0), None
    for head in range(heads + 1):
        upcoming = score(head + 1) if head + 1 < heads else None
        weighed = weigh(scores, head) if head < heads else None
        if ready is not None:
            finish(head - 1, *ready)
        scores, ready = upcoming, weighed
    if last:
        copies = []
        for i in range(2):
            here = slice(i * band // 2, (i + 1) * band // 2)
            out_work[here, :] = (
                jnp.dot(mixed[here, :], wo[...], preferred_element_type=F32) + bias[...][None, :]
            ).astype(BF)
            copies.append(pltpu.make_async_copy(out_work.at[here], out.at[here], out_sem.at[i]))
            copies[-1].start()
        for copy in copies + [hidden_copy]:
            copy.wait()


def attend(sources, wk, wv, query, state=None, final=None):
    channels = wk.shape[0]
    heads = channels // HD
    band = sources[0].shape[0] if state is None else query.shape[0]
    tokens = sum(source.shape[0] for source in sources)
    if state is None:
        tokens -= sources[2].shape[0]
    shape = jax.ShapeDtypeStruct
    carried = shape((heads, band, LANES), F32)
    square = shape((channels, channels), BF)
    scratch = [
        pltpu.VMEM((channels - HD + LANES, tokens), BF),
        pltpu.VMEM((heads * LANES, tokens), BF),
    ]
    operands = list(sources) + [wk, wv, query] + list(state or ()) + list(final or ())
    place = pltpu.VMEM
    if state is not None and final is not None:
        outs = (shape((band, channels), BF), shape((band, channels), BF))
        scratch += [
            pltpu.VMEM((band, heads * LANES), BF),
            pltpu.VMEM((band, channels), BF),
            pltpu.SemaphoreType.DMA((2,)),
            pltpu.SemaphoreType.DMA,
        ]
        place = pltpu.HBM
    elif state is None:
        scratch.append(pltpu.VMEM((tokens - 2 * band, channels), BF))
        outs = (
            carried,
            carried,
            square,
            square,
            shape((band, heads * LANES), BF),
            shape((heads * LANES, channels), BF),
        )
    else:
        outs = (carried, carried)
    return vmem_call(
        functools.partial(
            attend_kernel, len(sources), state is None, state is not None and final is not None
        ),
        outs,
        scratch,
        *operands,
        place=place,
    )


def swap(value, axis, bit):
    size = lax.axis_size(axis)
    return lax.ppermute(value, axis, [(i, i ^ bit) for i in range(size)])


def shards(frames, conv_weight, conv_bias, ref_features, w_query, w_key, w_value, w_out, out_bias):
    count, band_rows, width, channels = frames.shape
    band = band_rows * width
    x = frames.reshape(count * band, channels)
    tm, rows = lax.axis_size("tm"), lax.axis_size("rows")
    own = ref_features
    bit = tm // 2
    while bit > 4:
        own = jnp.concatenate([own, swap(own, "tm", bit)])
        bit //= 2
    core_row, first, own, far_half = sending(x, own, width)
    inner = range(1, rows - 1)
    partner = {i: i + 1 if i % 2 else i - 1 for i in inner}
    everyone = [(t, r) for t in range(tm) for r in range(rows)]
    far_half = swap(far_half, "tm", 4)
    first = lax.ppermute(
        first,
        ("tm", "rows"),
        [
            (t * rows + r, t * rows + partner[r] if r in partner else (t ^ 2) * rows + r)
            for t, r in everyone
        ],
    )
    core_row = swap(core_row, "rows", 1)
    total = opening(x, conv_weight, conv_bias, width)
    hidden = conv(core_row, first, total, conv_weight, width)
    pair = pairing(first, far_half, own)
    pair_core = swap(pair, "rows", 1)
    hidden_core = swap(hidden, "rows", 1)
    corner_half = swap(far_half, "tm", 2)
    last_half = swap(far_half, "tm", 3)
    beside = swap(pair, "tm", 1)
    hidden_y = swap(hidden, "rows", 2)
    *state, wk, wv, query, wo = attend(
        [hidden, hidden_core, own, pair, pair_core], w_key, w_value, w_query, final=(w_out,)
    )
    state, hidden_y, beside, corner_half, last_half = lax.optimization_barrier(
        (state, hidden_y, beside, corner_half, last_half)
    )
    across = jnp.concatenate([beside, corner_half])
    hidden_far = swap(hidden_y, "rows", 1)
    across_core = swap(jnp.concatenate([across, last_half]), "rows", 1)
    state = attend([hidden_y, across], wk, wv, query, state)
    attended, hidden = attend(
        [hidden_far, jnp.concatenate([across_core, last_half])],
        wk,
        wv,
        query,
        state,
        (wo, out_bias, hidden),
    )
    return (
        hidden.reshape(count, band_rows, width, channels),
        attended.reshape(count, band_rows, width, channels),
    )


def solution(mesh):
    return jax.shard_map(
        shards,
        mesh=mesh,
        in_specs=(P("tm", "rows", None, None), P(), P(), P("tm", None), P(), P(), P(), P(), P()),
        out_specs=(P("tm", "rows", None, None), P("tm", "rows", None, None)),
        check_vma=False,
    )
```

```python
import functools

import jax
import jax.numpy as jnp
from jax import lax
from jax.experimental import pallas as pl
from jax.experimental.pallas import tpu as pltpu
from jax.sharding import PartitionSpec as P

HD = 80
LANES = 128
SCALE = HD ** (-0.5) * 1.4426950408889634
BF = jnp.bfloat16
F32 = jnp.float32
VMEM_LIMIT = 24 << 20
LONG = pl.CostEstimate(flops=20 << 30, bytes_accessed=32 << 20, transcendentals=0)
COST = pl.CostEstimate(flops=1 << 10, bytes_accessed=1 << 10, transcendentals=0)


def vmem_call(body, outs, scratch, *operands, place=pltpu.VMEM):
    whole = pl.BlockSpec(memory_space=pltpu.VMEM)
    return pl.pallas_call(
        body,
        out_shape=outs,
        in_specs=[whole] * len(operands),
        out_specs=jax.tree.map(lambda _: pl.BlockSpec(memory_space=place), outs),
        scratch_shapes=scratch,
        cost_estimate=COST,
        compiler_params=pltpu.CompilerParams(vmem_limit_bytes=VMEM_LIMIT),
    )(*operands)


def silu(value):
    value = value.astype(F32)
    return value / (1.0 + jnp.exp(-value))


def shift_columns(active, width):
    rows = active.shape[0]
    column = lax.broadcasted_iota(jnp.int32, active.shape, 0) % width
    left = jnp.where(column == 0, 0.0, pltpu.roll(active, 1, 0))
    right = jnp.where(column == width - 1, 0.0, pltpu.roll(active, rows - 1, 0))
    return left.astype(BF), active.astype(BF), right.astype(BF)


def place():
    row = lax.axis_index("rows")
    return row % 2 == 0, (row > 0) & (row < lax.axis_size("rows") - 1)


def sending_kernel(
    x_in, ref_in, core_out, first_out, own_out, half_out, rows, row_sem, ref_sem
):
    width = core_out.shape[0]
    band = x_in.shape[0]
    copies = [
        pltpu.make_async_copy(x_in.at[:width], rows.at[0], row_sem.at[0]),
        pltpu.make_async_copy(x_in.at[band - width :], rows.at[1], row_sem.at[1]),
        pltpu.make_async_copy(ref_in, own_out, ref_sem),
    ]
    for copy in copies:
        copy.start()
    for copy in copies:
        copy.wait()
    is_first, is_inner = place()
    first, last = rows[0], rows[1]
    core_out[...] = jnp.where(is_first, last, first)
    own = own_out[...]
    half = half_out.shape[0]
    half_out[...] = jnp.where(is_first, own[:half], own[half:])
    first_out[...] = own
    first_out[:width] = jnp.where(is_inner, jnp.where(is_first, first, last), own[:width])


def sending(x, ref, width):
    channels = x.shape[1]
    shape = jax.ShapeDtypeStruct
    near = pl.BlockSpec(memory_space=pltpu.VMEM)
    far = pl.BlockSpec(memory_space=pltpu.HBM)
    return pl.pallas_call(
        sending_kernel,
        out_shape=(
            shape((width, channels), BF),
            shape(ref.shape, BF),
            shape(ref.shape, BF),
            shape((ref.shape[0] // 2, channels), BF),
        ),
        in_specs=[far, far],
        out_specs=(near,) * 4,
        scratch_shapes=[
            pltpu.VMEM((2, width, channels), BF),
            pltpu.SemaphoreType.DMA((2,)),
            pltpu.SemaphoreType.DMA,
        ],
        cost_estimate=LONG,
        compiler_params=pltpu.CompilerParams(vmem_limit_bytes=4 << 20),
    )(*[pltpu.with_memory_space_constraint(v, pltpu.HBM) for v in (x, ref)])


def opening_kernel(width, x, weight, bias, total_out, shifted):
    band, channels = x.shape
    for col, part in enumerate(shift_columns(silu(x[...]), width)):
        shifted[:, col * channels : (col + 1) * channels] = part
    taps = 3 * channels
    total_out[...] = (
        x[...].astype(F32)
        + bias[...][None, :]
        + jnp.dot(shifted[...], weight[1].reshape(taps, channels), preferred_element_type=F32)
    )
    total_out[width:, :] += jnp.dot(
        shifted[: band - width, :],
        weight[0].reshape(taps, channels),
        preferred_element_type=F32,
    )
    total_out[: band - width, :] += jnp.dot(
        shifted[width:, :], weight[2].reshape(taps, channels), preferred_element_type=F32
    )


def opening(x, weight, bias, width):
    band, channels = x.shape
    return vmem_call(
        functools.partial(opening_kernel, width),
        jax.ShapeDtypeStruct((band, channels), F32),
        [pltpu.VMEM((band, 3 * channels), BF)],
        x,
        weight,
        bias,
    )


def conv_kernel(
    width, core_row, cross_row, total, weight, hidden_out
):
    band, channels = total.shape
    is_first, is_inner = place()
    core_part = core_row[...]
    cross_part = jnp.where(is_inner, cross_row[:width], jnp.zeros_like(core_part))
    above = shift_columns(silu(jnp.where(is_first, cross_part, core_part)), width)
    below = shift_columns(silu(jnp.where(is_first, core_part, cross_part)), width)
    top, bottom = total[:width], total[band - width :]
    for col in range(3):
        top = top + jnp.dot(above[col], weight[0, col], preferred_element_type=F32)
        bottom = bottom + jnp.dot(below[col], weight[2, col], preferred_element_type=F32)
    hidden_out[width : band - width] = total[width : band - width].astype(BF)
    hidden_out[:width] = top.astype(BF)
    hidden_out[band - width :] = bottom.astype(BF)


def conv(core_row, cross_row, total, weight, width):
    near = pl.BlockSpec(memory_space=pltpu.VMEM)
    return pl.pallas_call(
        functools.partial(conv_kernel, width),
        out_shape=jax.ShapeDtypeStruct(total.shape, BF),
        in_specs=[near] * 4,
        out_specs=near,
        cost_estimate=COST,
        compiler_params=pltpu.CompilerParams(vmem_limit_bytes=VMEM_LIMIT),
    )(core_row, cross_row, total, weight)


def pairing_kernel(first, far_half, own, pair):
    _, is_inner = place()
    block = own.shape[0]
    pair[:block] = jnp.where(is_inner, own[...], first[...])
    pair[block:] = far_half[...]


def pairing(first, far_half, own):
    rows = own.shape[0] + far_half.shape[0]
    shape = jax.ShapeDtypeStruct((rows, own.shape[1]), BF)
    return vmem_call(pairing_kernel, shape, [], first, far_half, own)


def attend_kernel(pieces, first, last, *refs):
    refs = list(refs)
    sources = [refs.pop(0) for _ in range(pieces)]
    wk, wv, query = [refs.pop(0) for _ in range(3)]
    channels = wk.shape[0]
    heads = channels // HD
    if first:
        wo, top_out, sum_out, wk_out, wv_out, query_out, wo_out, keys, values, column = refs
        wo_out[...] = jnp.zeros_like(wo_out)
        for head in range(heads):
            wo_out[head * LANES : head * LANES + HD, :] = wo[head * HD : (head + 1) * HD, :]
        own, pair, pair_core = sources[2:]
        _, is_inner = place()
        block = own.shape[0]
        column[:block] = own[...]
        column[block : 2 * block] = jnp.where(is_inner, pair_core[:block], pair[:block])
        middle = 2 * block + pair.shape[0] - block
        column[2 * block : middle] = pair[block:]
        column[middle:] = pair_core[block:]
        sources = sources[:2] + [column]
        wk_out[...] = wk[...].T
        wv_out[...] = wv[...].T
        projected = (
            jnp.dot(sources[0][...], query[...], preferred_element_type=F32) * SCALE
        ).astype(BF)
        query_out[...] = jnp.zeros_like(query_out)
        for head in range(heads):
            query_out[:, head * LANES : head * LANES + HD] = projected[
                :, head * HD : (head + 1) * HD
            ]
        wk, wv, query = wk_out, wv_out, query_out
    else:
        top_in, sum_in = refs.pop(0), refs.pop(0)
        if last:
            wo, bias, hidden, out, hidden_out, keys, values, mixed, out_work, out_sem, hidden_sem = refs
            hidden_copy = pltpu.make_async_copy(hidden, hidden_out, hidden_sem)
            hidden_copy.start()
        else:
            top_out, sum_out, keys, values = refs
    band = query.shape[0]
    tokens = keys.shape[1]
    keys[channels:, :] = jnp.zeros((keys.shape[0] - channels, tokens), BF)
    start = 0
    for source in sources:
        part = source[...]
        length = part.shape[0]
        here = slice(start, start + length)
        contract = (((1,), (1,)), ((), ()))
        keys[:channels, here] = lax.dot_general(
            wk[...], part, contract, preferred_element_type=F32
        ).astype(BF)
        value = lax.dot_general(wv[...], part, contract, preferred_element_type=F32).astype(BF)
        for head in range(heads):
            values[head * LANES : head * LANES + HD, here] = value[head * HD : (head + 1) * HD]
            values[head * LANES + HD : (head + 1) * LANES, here] = jnp.ones(
                (LANES - HD, length), BF
            )
        start += length

    def score(head):
        return jnp.dot(
            query[:, head * LANES : (head + 1) * LANES],
            keys[head * HD : head * HD + LANES, :],
            preferred_element_type=F32,
        )

    def weigh(scores, head):
        top = jnp.broadcast_to(jnp.max(scores, axis=1, keepdims=True), (band, LANES))
        if not first:
            top = jnp.maximum(top, top_in[head])
        weights = jnp.concatenate(
            [
                jnp.exp2(scores[:, at : at + LANES] - top).astype(BF)
                for at in range(0, tokens, LANES)
            ],
            axis=1,
        )
        return top, weights

    def finish(head, top, weights):
        product = lax.dot_general(
            weights,
            values[head * LANES : (head + 1) * LANES, :],
            (((1,), (1,)), ((), ())),
            preferred_element_type=F32,
        )
        if not first:
            product = product + sum_in[head] * jnp.exp2(top_in[head] - top)
        if last:
            mixed[:, head * LANES : (head + 1) * LANES] = (
                product / product[:, HD : HD + 1]
            ).astype(BF)
        else:
            top_out[head] = top
            sum_out[head] = product

    scores, ready = score(0), None
    for head in range(heads + 1):
        upcoming = score(head + 1) if head + 1 < heads else None
        weighed = weigh(scores, head) if head < heads else None
        if ready is not None:
            finish(head - 1, *ready)
        scores, ready = upcoming, weighed
    if last:
        copies = []
        for i in range(2):
            here = slice(i * band // 2, (i + 1) * band // 2)
            out_work[here, :] = (
                jnp.dot(mixed[here, :], wo[...], preferred_element_type=F32) + bias[...][None, :]
            ).astype(BF)
            copies.append(pltpu.make_async_copy(out_work.at[here], out.at[here], out_sem.at[i]))
            copies[-1].start()
        for copy in copies + [hidden_copy]:
            copy.wait()


def attend(sources, wk, wv, query, state=None, final=None):
    channels = wk.shape[0]
    heads = channels // HD
    band = sources[0].shape[0] if state is None else query.shape[0]
    tokens = sum(source.shape[0] for source in sources)
    if state is None:
        tokens -= sources[2].shape[0]
    shape = jax.ShapeDtypeStruct
    carried = shape((heads, band, LANES), F32)
    square = shape((channels, channels), BF)
    scratch = [
        pltpu.VMEM((channels - HD + LANES, tokens), BF),
        pltpu.VMEM((heads * LANES, tokens), BF),
    ]
    operands = list(sources) + [wk, wv, query] + list(state or ()) + list(final or ())
    place = pltpu.VMEM
    if state is not None and final is not None:
        outs = (shape((band, channels), BF), shape((band, channels), BF))
        scratch += [
            pltpu.VMEM((band, heads * LANES), BF),
            pltpu.VMEM((band, channels), BF),
            pltpu.SemaphoreType.DMA((2,)),
            pltpu.SemaphoreType.DMA,
        ]
        place = pltpu.HBM
    elif state is None:
        scratch.append(pltpu.VMEM((tokens - 2 * band, channels), BF))
        outs = (
            carried,
            carried,
            square,
            square,
            shape((band, heads * LANES), BF),
            shape((heads * LANES, channels), BF),
        )
    else:
        outs = (carried, carried)
    return vmem_call(
        functools.partial(
            attend_kernel, len(sources), state is None, state is not None and final is not None
        ),
        outs,
        scratch,
        *operands,
        place=place,
    )


def swap(value, axis, bit):
    size = lax.axis_size(axis)
    return lax.ppermute(value, axis, [(i, i ^ bit) for i in range(size)])


def shards(frames, conv_weight, conv_bias, ref_features, w_query, w_key, w_value, w_out, out_bias):
    count, band_rows, width, channels = frames.shape
    band = band_rows * width
    x = frames.reshape(count * band, channels)
    tm, rows = lax.axis_size("tm"), lax.axis_size("rows")
    own = ref_features
    bit = tm // 2
    while bit > 4:
        own = jnp.concatenate([own, swap(own, "tm", bit)])
        bit //= 2
    core_row, first, own, far_half = sending(x, own, width)
    inner = range(1, rows - 1)
    partner = {i: i + 1 if i % 2 else i - 1 for i in inner}
    everyone = [(t, r) for t in range(tm) for r in range(rows)]
    far_half = swap(far_half, "tm", 4)
    first = lax.ppermute(
        first,
        ("tm", "rows"),
        [
            (t * rows + r, t * rows + partner[r] if r in partner else (t ^ 2) * rows + r)
            for t, r in everyone
        ],
    )
    core_row = swap(core_row, "rows", 1)
    total = opening(x, conv_weight, conv_bias, width)
    hidden = conv(core_row, first, total, conv_weight, width)
    pair = pairing(first, far_half, own)
    pair_core = swap(pair, "rows", 1)
    hidden_core = swap(hidden, "rows", 1)
    corner_half = swap(far_half, "tm", 2)
    last_half = swap(far_half, "tm", 3)
    beside = swap(pair, "tm", 1)
    hidden_y = swap(hidden, "rows", 2)
    *state, wk, wv, query, wo = attend(
        [hidden, hidden_core, own, pair, pair_core], w_key, w_value, w_query, final=(w_out,)
    )
    state, hidden_y, beside, corner_half, last_half = lax.optimization_barrier(
        (state, hidden_y, beside, corner_half, last_half)
    )
    across = jnp.concatenate([beside, corner_half])
    hidden_far = swap(hidden_y, "rows", 1)
    across_core = swap(jnp.concatenate([across, last_half]), "rows", 1)
    state = attend([hidden_y, across], wk, wv, query, state)
    attended, hidden = attend(
        [hidden_far, jnp.concatenate([across_core, last_half])],
        wk,
        wv,
        query,
        state,
        (wo, out_bias, hidden),
    )
    return (
        hidden.reshape(count, band_rows, width, channels),
        attended.reshape(count, band_rows, width, channels),
    )


def solution(mesh):
    return jax.shard_map(
        shards,
        mesh=mesh,
        in_specs=(P("tm", "rows", None, None), P(), P(), P("tm", None), P(), P(), P(), P(), P()),
        out_specs=(P("tm", "rows", None, None), P("tm", "rows", None, None)),
        check_vma=False,
    )
```

```python
import functools

import jax
import jax.numpy as jnp
from jax import lax
from jax.experimental import pallas as pl
from jax.experimental.pallas import tpu as pltpu
from jax.sharding import PartitionSpec as P

HD = 80
LANES = 128
SCALE = HD ** (-0.5) * 1.4426950408889634
BF = jnp.bfloat16
F32 = jnp.float32
VMEM_LIMIT = 24 << 20
LONG = pl.CostEstimate(flops=20 << 30, bytes_accessed=32 << 20, transcendentals=0)
COST = pl.CostEstimate(flops=1 << 10, bytes_accessed=1 << 10, transcendentals=0)


def vmem_call(body, outs, scratch, *operands, place=pltpu.VMEM):
    whole = pl.BlockSpec(memory_space=pltpu.VMEM)
    return pl.pallas_call(
        body,
        out_shape=outs,
        in_specs=[whole] * len(operands),
        out_specs=jax.tree.map(lambda _: pl.BlockSpec(memory_space=place), outs),
        scratch_shapes=scratch,
        cost_estimate=COST,
        compiler_params=pltpu.CompilerParams(vmem_limit_bytes=VMEM_LIMIT),
    )(*operands)


def silu(value):
    value = value.astype(F32)
    return value / (1.0 + jnp.exp(-value))


def shift_columns(active, width):
    rows = active.shape[0]
    column = lax.broadcasted_iota(jnp.int32, active.shape, 0) % width
    left = jnp.where(column == 0, 0.0, pltpu.roll(active, 1, 0))
    right = jnp.where(column == width - 1, 0.0, pltpu.roll(active, rows - 1, 0))
    return left.astype(BF), active.astype(BF), right.astype(BF)


def place():
    row = lax.axis_index("rows")
    return row % 2 == 0, (row > 0) & (row < lax.axis_size("rows") - 1)


def sending_kernel(
    x_in, ref_in, core_out, first_out, own_out, half_out, rows, row_sem, ref_sem
):
    width = core_out.shape[0]
    band = x_in.shape[0]
    copies = [
        pltpu.make_async_copy(x_in.at[:width], rows.at[0], row_sem.at[0]),
        pltpu.make_async_copy(x_in.at[band - width :], rows.at[1], row_sem.at[1]),
        pltpu.make_async_copy(ref_in, own_out, ref_sem),
    ]
    for copy in copies:
        copy.start()
    for copy in copies:
        copy.wait()
    is_first, is_inner = place()
    first, last = rows[0], rows[1]
    core_out[...] = jnp.where(is_first, last, first)
    own = own_out[...]
    half = half_out.shape[0]
    half_out[...] = jnp.where(is_first, own[:half], own[half:])
    first_out[...] = own
    first_out[:width] = jnp.where(is_inner, jnp.where(is_first, first, last), own[:width])


def sending(x, ref, width):
    channels = x.shape[1]
    shape = jax.ShapeDtypeStruct
    near = pl.BlockSpec(memory_space=pltpu.VMEM)
    far = pl.BlockSpec(memory_space=pltpu.HBM)
    return pl.pallas_call(
        sending_kernel,
        out_shape=(
            shape((width, channels), BF),
            shape(ref.shape, BF),
            shape(ref.shape, BF),
            shape((ref.shape[0] // 2, channels), BF),
        ),
        in_specs=[far, far],
        out_specs=(near,) * 4,
        scratch_shapes=[
            pltpu.VMEM((2, width, channels), BF),
            pltpu.SemaphoreType.DMA((2,)),
            pltpu.SemaphoreType.DMA,
        ],
        cost_estimate=LONG,
        compiler_params=pltpu.CompilerParams(vmem_limit_bytes=4 << 20),
    )(*[pltpu.with_memory_space_constraint(v, pltpu.HBM) for v in (x, ref)])


def shifting_kernel(width, x, shifted):
    channels = x.shape[1]
    for col, part in enumerate(shift_columns(silu(x[...]), width)):
        shifted[:, col * channels : (col + 1) * channels] = part


def opening_kernel(width, x, shifted, weight, bias, total_out):
    band, channels = x.shape
    taps = 3 * channels
    total_out[...] = (
        x[...].astype(F32)
        + bias[...][None, :]
        + jnp.dot(shifted[...], weight[1].reshape(taps, channels), preferred_element_type=F32)
    )
    total_out[width:, :] += jnp.dot(
        shifted[: band - width, :],
        weight[0].reshape(taps, channels),
        preferred_element_type=F32,
    )
    total_out[: band - width, :] += jnp.dot(
        shifted[width:, :], weight[2].reshape(taps, channels), preferred_element_type=F32
    )


def opening(x, weight, bias, width):
    band, channels = x.shape
    shape = jax.ShapeDtypeStruct
    shifted = vmem_call(
        functools.partial(shifting_kernel, width), shape((band, 3 * channels), BF), [], x
    )
    return vmem_call(
        functools.partial(opening_kernel, width),
        shape((band, channels), F32),
        [],
        x,
        shifted,
        weight,
        bias,
    )


def conv_kernel(
    width, core_row, cross_row, total, weight, hidden_out
):
    band, channels = total.shape
    is_first, is_inner = place()
    core_part = core_row[...]
    cross_part = jnp.where(is_inner, cross_row[:width], jnp.zeros_like(core_part))
    above = shift_columns(silu(jnp.where(is_first, cross_part, core_part)), width)
    below = shift_columns(silu(jnp.where(is_first, core_part, cross_part)), width)
    top, bottom = total[:width], total[band - width :]
    for col in range(3):
        top = top + jnp.dot(above[col], weight[0, col], preferred_element_type=F32)
        bottom = bottom + jnp.dot(below[col], weight[2, col], preferred_element_type=F32)
    hidden_out[width : band - width] = total[width : band - width].astype(BF)
    hidden_out[:width] = top.astype(BF)
    hidden_out[band - width :] = bottom.astype(BF)


def conv(core_row, cross_row, total, weight, width):
    near = pl.BlockSpec(memory_space=pltpu.VMEM)
    return pl.pallas_call(
        functools.partial(conv_kernel, width),
        out_shape=jax.ShapeDtypeStruct(total.shape, BF),
        in_specs=[near] * 4,
        out_specs=near,
        cost_estimate=COST,
        compiler_params=pltpu.CompilerParams(vmem_limit_bytes=VMEM_LIMIT),
    )(core_row, cross_row, total, weight)


def pairing_kernel(first, far_half, own, pair):
    _, is_inner = place()
    block = own.shape[0]
    pair[:block] = jnp.where(is_inner, own[...], first[...])
    pair[block:] = far_half[...]


def pairing(first, far_half, own):
    rows = own.shape[0] + far_half.shape[0]
    shape = jax.ShapeDtypeStruct((rows, own.shape[1]), BF)
    return vmem_call(pairing_kernel, shape, [], first, far_half, own)


def attend_kernel(pieces, first, last, *refs):
    refs = list(refs)
    sources = [refs.pop(0) for _ in range(pieces)]
    wk, wv, query = [refs.pop(0) for _ in range(3)]
    channels = wk.shape[0]
    heads = channels // HD
    if first:
        wo, top_out, sum_out, wk_out, wv_out, query_out, wo_out, keys, values, column = refs
        wo_out[...] = jnp.zeros_like(wo_out)
        for head in range(heads):
            wo_out[head * LANES : head * LANES + HD, :] = wo[head * HD : (head + 1) * HD, :]
        own, pair, pair_core = sources[2:]
        _, is_inner = place()
        block = own.shape[0]
        column[:block] = own[...]
        column[block : 2 * block] = jnp.where(is_inner, pair_core[:block], pair[:block])
        middle = 2 * block + pair.shape[0] - block
        column[2 * block : middle] = pair[block:]
        column[middle:] = pair_core[block:]
        sources = sources[:2] + [column]
        wk_out[...] = wk[...].T
        wv_out[...] = wv[...].T
        projected = (
            jnp.dot(sources[0][...], query[...], preferred_element_type=F32) * SCALE
        ).astype(BF)
        query_out[...] = jnp.zeros_like(query_out)
        for head in range(heads):
            query_out[:, head * LANES : head * LANES + HD] = projected[
                :, head * HD : (head + 1) * HD
            ]
        wk, wv, query = wk_out, wv_out, query_out
    else:
        top_in, sum_in = refs.pop(0), refs.pop(0)
        if last:
            wo, bias, hidden, out, hidden_out, keys, values, mixed, out_work, out_sem, hidden_sem = refs
            hidden_copy = pltpu.make_async_copy(hidden, hidden_out, hidden_sem)
            hidden_copy.start()
        else:
            top_out, sum_out, keys, values = refs
    band = query.shape[0]
    tokens = keys.shape[1]
    keys[channels:, :] = jnp.zeros((keys.shape[0] - channels, tokens), BF)
    start = 0
    for source in sources:
        part = source[...]
        length = part.shape[0]
        here = slice(start, start + length)
        contract = (((1,), (1,)), ((), ()))
        keys[:channels, here] = lax.dot_general(
            wk[...], part, contract, preferred_element_type=F32
        ).astype(BF)
        value = lax.dot_general(wv[...], part, contract, preferred_element_type=F32).astype(BF)
        for head in range(heads):
            values[head * LANES : head * LANES + HD, here] = value[head * HD : (head + 1) * HD]
            values[head * LANES + HD : (head + 1) * LANES, here] = jnp.ones(
                (LANES - HD, length), BF
            )
        start += length

    def score(head):
        return jnp.dot(
            query[:, head * LANES : (head + 1) * LANES],
            keys[head * HD : head * HD + LANES, :],
            preferred_element_type=F32,
        )

    def weigh(scores, head):
        top = jnp.broadcast_to(jnp.max(scores, axis=1, keepdims=True), (band, LANES))
        if not first:
            top = jnp.maximum(top, top_in[head])
        weights = jnp.concatenate(
            [
                jnp.exp2(scores[:, at : at + LANES] - top).astype(BF)
                for at in range(0, tokens, LANES)
            ],
            axis=1,
        )
        return top, weights

    def finish(head, top, weights):
        product = lax.dot_general(
            weights,
            values[head * LANES : (head + 1) * LANES, :],
            (((1,), (1,)), ((), ())),
            preferred_element_type=F32,
        )
        if not first:
            product = product + sum_in[head] * jnp.exp2(top_in[head] - top)
        if last:
            mixed[:, head * LANES : (head + 1) * LANES] = (
                product / product[:, HD : HD + 1]
            ).astype(BF)
        else:
            top_out[head] = top
            sum_out[head] = product

    scores, ready = score(0), None
    for head in range(heads + 1):
        upcoming = score(head + 1) if head + 1 < heads else None
        weighed = weigh(scores, head) if head < heads else None
        if ready is not None:
            finish(head - 1, *ready)
        scores, ready = upcoming, weighed
    if last:
        copies = []
        for i in range(2):
            here = slice(i * band // 2, (i + 1) * band // 2)
            out_work[here, :] = (
                jnp.dot(mixed[here, :], wo[...], preferred_element_type=F32) + bias[...][None, :]
            ).astype(BF)
            copies.append(pltpu.make_async_copy(out_work.at[here], out.at[here], out_sem.at[i]))
            copies[-1].start()
        for copy in copies + [hidden_copy]:
            copy.wait()


def attend(sources, wk, wv, query, state=None, final=None):
    channels = wk.shape[0]
    heads = channels // HD
    band = sources[0].shape[0] if state is None else query.shape[0]
    tokens = sum(source.shape[0] for source in sources)
    if state is None:
        tokens -= sources[2].shape[0]
    shape = jax.ShapeDtypeStruct
    carried = shape((heads, band, LANES), F32)
    square = shape((channels, channels), BF)
    scratch = [
        pltpu.VMEM((channels - HD + LANES, tokens), BF),
        pltpu.VMEM((heads * LANES, tokens), BF),
    ]
    operands = list(sources) + [wk, wv, query] + list(state or ()) + list(final or ())
    place = pltpu.VMEM
    if state is not None and final is not None:
        outs = (shape((band, channels), BF), shape((band, channels), BF))
        scratch += [
            pltpu.VMEM((band, heads * LANES), BF),
            pltpu.VMEM((band, channels), BF),
            pltpu.SemaphoreType.DMA((2,)),
            pltpu.SemaphoreType.DMA,
        ]
        place = pltpu.HBM
    elif state is None:
        scratch.append(pltpu.VMEM((tokens - 2 * band, channels), BF))
        outs = (
            carried,
            carried,
            square,
            square,
            shape((band, heads * LANES), BF),
            shape((heads * LANES, channels), BF),
        )
    else:
        outs = (carried, carried)
    return vmem_call(
        functools.partial(
            attend_kernel, len(sources), state is None, state is not None and final is not None
        ),
        outs,
        scratch,
        *operands,
        place=place,
    )


def swap(value, axis, bit):
    size = lax.axis_size(axis)
    return lax.ppermute(value, axis, [(i, i ^ bit) for i in range(size)])


def shards(frames, conv_weight, conv_bias, ref_features, w_query, w_key, w_value, w_out, out_bias):
    count, band_rows, width, channels = frames.shape
    band = band_rows * width
    x = frames.reshape(count * band, channels)
    tm, rows = lax.axis_size("tm"), lax.axis_size("rows")
    own = ref_features
    bit = tm // 2
    while bit > 4:
        own = jnp.concatenate([own, swap(own, "tm", bit)])
        bit //= 2
    core_row, first, own, far_half = sending(x, own, width)
    inner = range(1, rows - 1)
    partner = {i: i + 1 if i % 2 else i - 1 for i in inner}
    everyone = [(t, r) for t in range(tm) for r in range(rows)]
    far_half = swap(far_half, "tm", 4)
    first = lax.ppermute(
        first,
        ("tm", "rows"),
        [
            (t * rows + r, t * rows + partner[r] if r in partner else (t ^ 2) * rows + r)
            for t, r in everyone
        ],
    )
    core_row = swap(core_row, "rows", 1)
    total = opening(x, conv_weight, conv_bias, width)
    hidden = conv(core_row, first, total, conv_weight, width)
    pair = pairing(first, far_half, own)
    pair_core = swap(pair, "rows", 1)
    hidden_core = swap(hidden, "rows", 1)
    corner_half = swap(far_half, "tm", 2)
    last_half = swap(far_half, "tm", 3)
    beside = swap(pair, "tm", 1)
    hidden_y = swap(hidden, "rows", 2)
    *state, wk, wv, query, wo = attend(
        [hidden, hidden_core, own, pair, pair_core], w_key, w_value, w_query, final=(w_out,)
    )
    state, hidden_y, beside, corner_half, last_half = lax.optimization_barrier(
        (state, hidden_y, beside, corner_half, last_half)
    )
    across = jnp.concatenate([beside, corner_half])
    hidden_far = swap(hidden_y, "rows", 1)
    across_core = swap(jnp.concatenate([across, last_half]), "rows", 1)
    state = attend([hidden_y, across], wk, wv, query, state)
    attended, hidden = attend(
        [hidden_far, jnp.concatenate([across_core, last_half])],
        wk,
        wv,
        query,
        state,
        (wo, out_bias, hidden),
    )
    return (
        hidden.reshape(count, band_rows, width, channels),
        attended.reshape(count, band_rows, width, channels),
    )


def solution(mesh):
    return jax.shard_map(
        shards,
        mesh=mesh,
        in_specs=(P("tm", "rows", None, None), P(), P(), P("tm", None), P(), P(), P(), P(), P()),
        out_specs=(P("tm", "rows", None, None), P("tm", "rows", None, None)),
        check_vma=False,
    )
```
